32 devices in a mesh: ctx: 4 (over y, x), head: 8 (over z, core).
Axes of the slice: x: 2, y: 2, z: 4, core: 2. Of those that a mesh axis runs over, the one named last changes fastest.
Arguments:
- attn_in: bfloat16 [8192, 8192], P('ctx', 'head'), may hold values from -6 to 6
- w_key: bfloat16 [8192, 1024], P('head'), may hold values from -0.09375 to 0.09375
- w_value: bfloat16 [8192, 1024], P('head'), may hold values from -0.09375 to 0.09375
- ssm_in: bfloat16 [8192, 8192], P('ctx', 'head'), may hold values from -6 to 6
- gate: bfloat16 [8192, 8192], P('ctx', 'head'), may hold values from -6 to 6
- in_b: bfloat16 [8192, 256], P('ctx'), may hold values from -0.0234375 to 0.0234375
- in_c: bfloat16 [8192, 256], P('ctx'), may hold values from -6 to 6
- rate: float32 [128, 8192], P('head', 'ctx'), may hold values from 0 to 1
- skip: float32 [128], P('head'), may hold values from 0.5 to 2
- gain: float32 [8192], P('head'), may hold values from 0.5 to 1.5
- page_table: int32 [32, 8, 2], replicated, may hold values from 0 to 7, as said below
Outputs:
- mixer_out: bfloat16 [8192, 8192], P('ctx', 'head')
- kv_cache: bfloat16 [32, 2, 1024, 256], P('ctx', None, 'head')
- kv_scale: bfloat16 [32, 2, 16], P('ctx', None, 'head')
The draws below stay inside these ranges and needn't reach their ends.
Inputs may be any that keep to these rules, and one draw needn't show every extreme that they name: page_table[p, k] = (o, r): head k's columns of page p go to context index o (0 to 3), slot r (0 to 7). For each key-value head, one context shard sends at most 2 of its pages to one owner, and some shard exactly 2; every owner receives at most 8 pages and one owner exactly 8; an owner's slots are 0, 1, 2 and so on, in increasing order of the page's index in the prompt.
All inputs are finite; a program needn't handle non-finite values. Where the reference program divides by a largest or mean magnitude, that divisor is 1e-20 or more.
Results may differ from the reference program's by a relative error of at most 0.0053.
Values may be sent and summed in bfloat16 or wider, within the bound.
A program may use at most 192 MiB of HBM per device.

```python
import math
import jax
import jax.numpy as jnp
from jax import lax

D = 8192
NH = 128
P_SIZE = 64
STATE = 256
SPAN = 256
HD = 128
KVH = 8
PAGE = 256
GROUP = 64
TOK_DEV = 2048
INPUT_SEQ_COUNT = 8192
KVW = 1024
PAGES_DEV = 8
PAGES = 32
SLOTS = 8
N_CTX = 4


def draw_rate(key, part):
    key = jax.random.fold_in(key, 3)
    rapid_noise_seed, brisk_noise_seed, gradual_noise_seed, tile_noise_seed, coarse_noise_seed, flurry_noise_seed = jax.random.split(key, 6)
    share = 0.5
    fast = jax.random.uniform(rapid_noise_seed, (NH, 1)) < share
    quick = jnp.exp(jax.random.uniform(brisk_noise_seed, (NH, 1), minval=math.log(1.0 / 50.0), maxval=math.log(1.0 / 30.0)))
    slow = jnp.exp(jax.random.uniform(gradual_noise_seed, (NH, 1), minval=math.log(0.05), maxval=math.log(0.3))) / INPUT_SEQ_COUNT
    starting_level = jnp.where(fast, quick, slow)
    tile_scaling = jnp.exp(jax.random.uniform(tile_noise_seed, (NH, INPUT_SEQ_COUNT // TOK_DEV), minval=math.log(0.5), maxval=math.log(2.0)))
    tile_scaling = jnp.repeat(tile_scaling, TOK_DEV, axis=1)
    approximate_guess = jax.random.uniform(coarse_noise_seed, (NH, INPUT_SEQ_COUNT), minval=0.5, maxval=1.5)
    sampled_indices = jax.random.randint(flurry_noise_seed, (3,), 0, INPUT_SEQ_COUNT)
    flurry_extent = jnp.sum((jnp.arange(INPUT_SEQ_COUNT)[None, :] == sampled_indices[:, None]).astype(jnp.float32), axis=0) * 0.3
    return (starting_level * tile_scaling * approximate_guess + flurry_extent[None, :]).astype(jnp.float32)


def one_head_table(key):
    perm_key, busy_key, order_key, pick_key = jax.random.split(key, 4)
    cap_pages = (PAGES_DEV + N_CTX - 1) // N_CTX
    relabel = jax.random.permutation(perm_key, N_CTX)
    source_ids = jnp.arange(N_CTX)[:, None]
    page_ids = jnp.arange(PAGES_DEV)[None, :]
    starting_level = relabel[(source_ids * PAGES_DEV + page_ids) % N_CTX]
    busy = jax.random.randint(busy_key, (), 0, N_CTX)
    to_busy = jnp.sum((starting_level == busy).astype(jnp.int32), axis=1)
    free = to_busy < cap_pages
    order = jax.random.permutation(order_key, N_CTX)
    free_order = free[order].astype(jnp.int32)
    free_before = jnp.cumsum(free_order) - free_order
    chosen_order = jnp.logical_and(free_order == 1, free_before < SLOTS - PAGES_DEV)
    chosen = jnp.zeros((N_CTX,), jnp.bool_).at[order].set(chosen_order)
    scores = jax.random.randint(pick_key, (N_CTX, PAGES_DEV), 0, 1 << 20) * PAGES_DEV + page_ids
    masked = jnp.where(starting_level == busy, -1, scores)
    which_page = jnp.argmax(masked, axis=1)
    redirect = jnp.logical_and(chosen[:, None], page_ids == which_page[:, None])
    owners = jnp.where(redirect, busy, starting_level).astype(jnp.int32)
    flat = owners.reshape(PAGES)
    hits = (flat[:, None] == jnp.arange(N_CTX)[None, :]).astype(jnp.int32)
    before = jnp.cumsum(hits, axis=0) - hits
    slot_ids = jnp.sum(hits * before, axis=1).astype(jnp.int32)
    return jnp.stack([flat, slot_ids], axis=-1)


def draw_page_table(key, part):
    key = jax.random.fold_in(key, 7)
    head_keys = jax.random.split(key, KVH)
    tables = jax.vmap(one_head_table)(head_keys)
    return jnp.transpose(tables, (1, 0, 2)).astype(jnp.int32)


def with_spikes(array, key, source, target, shards_of, factor):
    owner, partner = [(jnp.arange(array.shape[position]) // (array.shape[position] // shards_of)).reshape([-1 if axis == position else 1 for axis in range(array.ndim)]) for position in (source, target)]
    chosen = jax.random.permutation(key, shards_of)[partner]
    strong = (owner == chosen) | (owner == (partner + shards_of // 2) % shards_of)
    return jnp.where(strong, factor * array, array)


def steps_of(stream_key, shape, shards, smallest, top_value):
    level = 1.0
    for dim, blocks in shards:
        heights = jax.random.uniform(jax.random.fold_in(jax.random.fold_in(stream_key, 6), dim), (blocks,), jnp.float32, smallest / len(shards), top_value / len(shards))
        level = level * jnp.repeat(jnp.exp(heights), shape[dim] // blocks).reshape((-1,) + (1,) * (len(shape) - 1 - dim))
    return level


def bell_draw(rng, extent, scale, reach, cuts=(), kind=jnp.bfloat16):
    result = jax.random.normal(rng, extent, jnp.float32) * scale
    if len(cuts) > 0:
        result = steps_of(rng, extent, cuts, -0.22, 0.18) * result
    return jnp.clip(result, min=-reach, max=reach).astype(kind)


def bell_draw_with(key, dims, width, most, cuts, heavy, held_as=jnp.bfloat16):
    values = width * jax.random.normal(key, dims, jnp.float32)
    if cuts:
        values = values * steps_of(key, dims, cuts, -0.22, 0.18)
    return jnp.clip(with_spikes(values, jax.random.fold_in(key, 3), *heavy), -most, most).astype(held_as)


def setup_inputs(seed: int = 0) -> dict:
    key_list = jax.random.split(jax.random.key(seed), 12)
    return {
        "attn_in": bell_draw(key_list[0], (INPUT_SEQ_COUNT, D), 1.0, 6.0, ((0, 4), (1, 8))),
        "w_key": bell_draw_with(key_list[1], (D, KVW), D ** -0.5, 0.09375, ((0, 8),), (0, 1, 8, 2.0)),
        "w_value": bell_draw_with(key_list[2], (D, KVW), D ** -0.5, 0.09375, ((0, 8),), (0, 1, 8, 2.0)),
        "ssm_in": bell_draw(key_list[3], (INPUT_SEQ_COUNT, NH * P_SIZE), 1.0, 6.0, ((0, 4), (1, 8))),
        "gate": bell_draw(key_list[4], (INPUT_SEQ_COUNT, NH * P_SIZE), 1.0, 6.0, ((0, 4), (1, 8))),
        "in_b": bell_draw(key_list[5], (INPUT_SEQ_COUNT, STATE), (STATE * SPAN) ** -0.5, 0.0234375, ((0, 4),)),
        "in_c": bell_draw(key_list[6], (INPUT_SEQ_COUNT, STATE), 1.0, 6.0, ((0, 4),)),
        "rate": draw_rate(jax.random.fold_in(key_list[11], 71), 0),
        "skip": jnp.clip(0.5 + 1.5 * jax.random.uniform(key_list[8], (NH,), jnp.float32) ** steps_of(key_list[8], (NH,), ((0, 8),), -0.2, 0.2), 0.5, 2.0),
        "gain": jnp.clip(0.5 + 1.0 * jax.random.uniform(key_list[9], (NH * P_SIZE,), jnp.float32) ** steps_of(key_list[9], (NH * P_SIZE,), ((0, 8),), -0.2, 0.2), 0.5, 1.5),
        "page_table": draw_page_table(jax.random.fold_in(key_list[11], 71), 0),
    }


def reference(attn_in, w_key, w_value, ssm_in, gate, in_b, in_c, rate, skip, gain, page_table):
    span_count = INPUT_SEQ_COUNT // SPAN
    cumulative = jnp.cumsum((-rate).reshape(NH, span_count, SPAN), axis=2)
    causal = jnp.arange(SPAN)[:, None] >= jnp.arange(SPAN)[None, :]

    def span_pass(entering, span_data):
        x_span, b_span, c_span, cum_span = span_data
        cross = jnp.dot(c_span, b_span.T, preferred_element_type=jnp.float32)
        spread = cum_span[:, :, None] - cum_span[:, None, :]
        mixing = (cross[None] * jnp.exp(jnp.where(causal[None], spread, -1e+30))).astype(jnp.bfloat16)
        mixing = lax.optimization_barrier(mixing)
        x_wide = x_span.astype(jnp.float32)
        diag_part = jnp.einsum('hqk,khp->qhp', mixing.astype(jnp.float32), x_wide)
        span_total = cum_span[:, -1]
        decayed = (x_wide * jnp.exp(span_total[:, None] - cum_span).T[:, :, None]).astype(jnp.bfloat16)
        decayed = lax.optimization_barrier(decayed)
        span_state = jnp.einsum('kn,khp->hnp', b_span.astype(jnp.float32), decayed.astype(jnp.float32))
        entering_b = lax.optimization_barrier(entering.astype(jnp.bfloat16))
        carried_part = jnp.einsum('qn,hnp->qhp', c_span.astype(jnp.float32), entering_b.astype(jnp.float32))
        carried_part = carried_part * jnp.exp(cum_span).T[:, :, None]
        output_sum = diag_part + carried_part + skip[None, :, None] * x_wide
        leaving = jnp.exp(span_total)[:, None, None] * entering + span_state
        return (leaving, output_sum)
    span_data = (ssm_in.reshape(span_count, SPAN, NH, P_SIZE), in_b.reshape(span_count, SPAN, STATE), in_c.reshape(span_count, SPAN, STATE), cumulative.transpose(1, 0, 2))
    start_state = jnp.zeros((NH, STATE, P_SIZE), jnp.float32)
    final_state, outputs = lax.scan(span_pass, start_state, span_data)
    mixed = outputs.reshape(INPUT_SEQ_COUNT, NH * P_SIZE)
    gated_out = mixed * jax.nn.silu(gate.astype(jnp.float32))
    mean_square = lax.optimization_barrier(jnp.mean(gated_out * gated_out, axis=1, keepdims=True))
    mixer_out = (gated_out * lax.rsqrt(mean_square + 1e-05) * gain[None, :]).astype(jnp.bfloat16)
    keys = jnp.dot(attn_in, w_key, preferred_element_type=jnp.float32)
    values = jnp.dot(attn_in, w_value, preferred_element_type=jnp.float32)
    group_count = KVW // GROUP
    both = jnp.stack([keys, values], axis=0).reshape(2, PAGES, PAGE, group_count, GROUP)
    page_max = lax.optimization_barrier(jnp.max(jnp.abs(both), axis=(2, 4)))
    quantized = (both / (page_max[:, :, None, :, None] + 1e-06)).astype(jnp.bfloat16)
    quantized = quantized.reshape(2, PAGES, PAGE, KVW).transpose(1, 0, 3, 2)
    by_head = quantized.reshape(PAGES, 2, KVH, HD, PAGE).transpose(0, 2, 1, 3, 4)
    row_count = N_CTX * SLOTS
    dest_rows = (page_table[:, :, 0] * SLOTS + page_table[:, :, 1]).astype(jnp.int32)
    head_ids = jnp.broadcast_to(jnp.arange(KVH, dtype=jnp.int32)[None, :], (PAGES, KVH))
    cache_heads = jnp.zeros((row_count, KVH, 2, HD, PAGE), jnp.bfloat16).at[dest_rows, head_ids].set(by_head)
    kv_cache = cache_heads.transpose(0, 2, 1, 3, 4).reshape(row_count, 2, KVW, PAGE)
    scale_heads = page_max.astype(jnp.bfloat16).transpose(1, 0, 2).reshape(PAGES, 2, KVH, HD // GROUP)
    scale_heads = scale_heads.transpose(0, 2, 1, 3)
    scale_rows = jnp.zeros((row_count, KVH, 2, HD // GROUP), jnp.bfloat16).at[dest_rows, head_ids].set(scale_heads)
    kv_scale = scale_rows.transpose(0, 2, 1, 3).reshape(row_count, 2, group_count)
    return (mixer_out, kv_cache, kv_scale)
```

```python
import jax
import jax.numpy as jnp
from jax import lax
from jax.sharding import PartitionSpec as P
from jax.experimental import pallas as pl
from jax.experimental.pallas import tpu as pltpu

NH = 128
P_SIZE = 64
SPAN = 256
HD = 128
PAGE = 256
GROUP = 64


LOG2E = 1.4426950408889634
F32 = jnp.float32


def lanes_of_pair(columns, p, lane_low):
    rows = columns.shape[0]
    first = jnp.broadcast_to(columns[:, 2 * p : 2 * p + 1], (rows, 2 * P_SIZE))
    second = jnp.broadcast_to(columns[:, 2 * p + 1 : 2 * p + 2], (rows, 2 * P_SIZE))
    return jnp.where(lane_low, first, second)


def state_kernel(x_ref, b_ref, col_ref, decay_ref, ent_ref, last_ref, run):
    k = pl.program_id(0)

    @pl.when(k == 0)
    def _():
        run[...] = jnp.zeros_like(run)

    ent_ref[0] = run[...]
    cum = col_ref[...]
    weights = jnp.exp2(cum[SPAN - 1 :, :] - cum)
    lane_low = lax.broadcasted_iota(jnp.int32, (SPAN, 2 * P_SIZE), 1) < P_SIZE
    b_t = b_ref[...].T
    for p in range(cum.shape[1] // 2):
        at = slice(p * 2 * P_SIZE, (p + 1) * 2 * P_SIZE)
        decayed = (x_ref[:, at].astype(F32) * lanes_of_pair(weights, p, lane_low)).astype(jnp.bfloat16)
        part = jnp.dot(b_t, decayed, preferred_element_type=F32)
        run[:, at] = run[:, at] * decay_ref[0, :, at] + part

    @pl.when(k == pl.num_programs(0) - 1)
    def _():
        last_ref[...] = run[...]


def mix_kernel(x_ref, g_ref, b_ref, c_ref, col_ref, row_ref, ent_ref, car_ref, bef_ref, skip_ref, o_ref, s_ref):
    c = c_ref[...]
    cross = lax.dot_general(c, b_ref[...], (((1,), (1,)), ((), ())), preferred_element_type=F32)
    t_at = lax.broadcasted_iota(jnp.int32, (SPAN, SPAN), 0)
    u_at = lax.broadcasted_iota(jnp.int32, (SPAN, SPAN), 1)
    cross = jnp.where(u_at <= t_at, cross, 0.0)
    cum = col_ref[...]
    leaving = jnp.exp2(cum)
    lane_low = lax.broadcasted_iota(jnp.int32, (SPAN, 2 * P_SIZE), 1) < P_SIZE
    total = jnp.zeros((SPAN, 2 * P_SIZE), F32)
    for p in range(cum.shape[1] // 2):
        at = slice(p * 2 * P_SIZE, (p + 1) * 2 * P_SIZE)
        x = x_ref[:, at].astype(F32)
        out = skip_ref[:, at] * x
        entering = (ent_ref[0, :, at] + bef_ref[0, :, at] * car_ref[:, at]).astype(jnp.bfloat16)
        out += lanes_of_pair(leaving, p, lane_low) * jnp.dot(c, entering, preferred_element_type=F32)
        for i in range(2):
            h = 2 * p + i
            spread = jnp.minimum(cum[:, h : h + 1] - row_ref[h : h + 1, :], 0.0)
            mixing = (cross * jnp.exp2(spread)).astype(jnp.bfloat16)
            mine = jnp.where(lane_low == (i == 0), x, 0.0).astype(jnp.bfloat16)
            out += jnp.dot(mixing, mine, preferred_element_type=F32)
        gate = g_ref[:, at].astype(F32)
        out = out * (gate / (1.0 + jnp.exp2(gate * -LOG2E)))
        o_ref[:, at] = out
        total += out * out
    s_ref[...] = jnp.sum(total, axis=1, keepdims=True)


def page_ranks(owner_rows):
    count = owner_rows.shape[-1]
    same = owner_rows[..., :, None] == owner_rows[..., None, :]
    earlier = jnp.arange(count)[None, :] < jnp.arange(count)[:, None]
    return jnp.sum(jnp.logical_and(same, earlier).astype(jnp.int32), axis=-1)


def body(attn_in, w_key, w_value, ssm_in, gate, in_b, in_c, rate, skip, gain, page_table):
    tok_rows, width = ssm_in.shape
    heads_local = rate.shape[0]
    state_dim = in_b.shape[1]
    head_count = lax.axis_size("head")
    ctx_count = lax.axis_size("ctx")
    spans = tok_rows // SPAN
    kv_width = w_key.shape[1] // head_count
    feature_rows = w_key.shape[0]
    w_both = jnp.stack(
        (
            w_key.reshape(feature_rows, head_count, kv_width),
            w_value.reshape(feature_rows, head_count, kv_width),
        ),
        axis=2,
    )
    w_both = w_both.reshape(feature_rows, head_count * 2 * kv_width)
    kv_part = lax.dot_general(
        w_both, attn_in, (((0,), (1,)), ((), ())), preferred_element_type=jnp.float32
    )
    kv_rows = lax.psum_scatter(kv_part, "head", scatter_dimension=0, tiled=True)

    upto = (jnp.arange(SPAN)[:, None] <= jnp.arange(SPAN)[None, :]).astype(F32)
    cum = jnp.einsum(
        "hcu,ut->hct", rate.reshape(heads_local, spans, SPAN) * -LOG2E, upto,
        precision=lax.Precision.HIGHEST,
    )
    span_total = cum[:, :, -1]
    cum_row = cum.reshape(heads_local, tok_rows)
    cum_col = cum_row.T
    before_span = jnp.cumsum(span_total, axis=1) - span_total

    def per_lane(values):
        return jnp.repeat(values, P_SIZE, axis=0).T.reshape(-1, 1, width)

    decay = per_lane(jnp.exp2(span_total))
    before = per_lane(jnp.exp2(before_span))
    rows = lambda w: pl.BlockSpec((SPAN, w), lambda k: (k, 0))
    lane_rows = pl.BlockSpec((1, 1, width), lambda k: (k, 0, 0))
    states = pl.BlockSpec((1, state_dim, width), lambda k: (k, 0, 0))
    whole = lambda *s: pl.BlockSpec(s, lambda k: (0,) * len(s))
    params = pltpu.CompilerParams(vmem_limit_bytes=48 * 1024 * 1024)
    entering, device_state = pl.pallas_call(
        state_kernel,
        grid=(spans,),
        in_specs=[rows(width), rows(state_dim), rows(heads_local), lane_rows],
        out_specs=[states, whole(state_dim, width)],
        out_shape=[
            jax.ShapeDtypeStruct((spans, state_dim, width), F32),
            jax.ShapeDtypeStruct((state_dim, width), F32),
        ],
        scratch_shapes=[pltpu.VMEM((state_dim, width), F32)],
        compiler_params=params,
        cost_estimate=pl.CostEstimate(flops=10**10, bytes_accessed=20 * 2**20, transcendentals=0),
    )(ssm_in, in_b, cum_col, decay)
    device_total = jnp.sum(span_total, axis=1)
    all_states = lax.all_gather(device_state, "ctx")
    all_totals = lax.all_gather(device_total, "ctx")
    place = lax.axis_index("ctx")
    earlier = jnp.arange(ctx_count) < place
    between = jnp.sum(
        jnp.where(
            ((jnp.arange(ctx_count)[None, :] > jnp.arange(ctx_count)[:, None]) & earlier[None, :])[:, :, None],
            all_totals[None],
            0.0,
        ),
        axis=1,
    )
    weight = jnp.where(earlier[:, None], jnp.exp2(between), 0.0)
    carried = jnp.sum(all_states * jnp.repeat(weight, P_SIZE, axis=1)[:, None, :], axis=0)
    gated_out, square_sum = pl.pallas_call(
        mix_kernel,
        grid=(spans,),
        in_specs=[
            rows(width), rows(width), rows(state_dim), rows(state_dim), rows(heads_local),
            pl.BlockSpec((heads_local, SPAN), lambda k: (0, k)),
            states, whole(state_dim, width), lane_rows, whole(1, width),
        ],
        out_specs=[rows(width), rows(1)],
        out_shape=[
            jax.ShapeDtypeStruct((tok_rows, width), F32),
            jax.ShapeDtypeStruct((tok_rows, 1), F32),
        ],
        compiler_params=params,
        cost_estimate=pl.CostEstimate(flops=3 * 10**10, bytes_accessed=40 * 2**20, transcendentals=0),
    )(ssm_in, gate, in_b, in_c, cum_col, cum_row, entering, carried, before,
      jnp.repeat(skip, P_SIZE).reshape(1, width))
    mean_square = lax.psum(square_sum[:, 0], "head") / (NH * P_SIZE)
    mixer_out = (gated_out * lax.rsqrt(mean_square + 1e-05)[:, None] * gain[None, :]).astype(
        jnp.bfloat16
    )
    pages_dev = tok_rows // PAGE
    groups = kv_width // GROUP
    by_page = kv_rows.reshape(2, kv_width, pages_dev, PAGE).transpose(2, 0, 1, 3)
    grouped = by_page.reshape(pages_dev, 2, groups, GROUP, PAGE)
    page_max = jnp.max(jnp.abs(grouped), axis=(3, 4))
    quantized = (grouped / (page_max[..., None, None] + 1e-06)).astype(jnp.bfloat16)
    quantized = quantized.reshape(pages_dev, 2, kv_width, PAGE)
    scale_part = page_max.astype(jnp.bfloat16)
    cap_pages = (pages_dev + ctx_count - 1) // ctx_count
    slot_count = min(ctx_count * cap_pages, 2 * pages_dev)
    ctx_index = lax.axis_index("ctx")
    kv_head = lax.axis_index("head") * kv_width // HD
    head_table = lax.dynamic_index_in_dim(page_table, kv_head, 1, keepdims=False)
    owners_all = head_table[:, 0].reshape(ctx_count, pages_dev)
    slots_all = head_table[:, 1].reshape(ctx_count, pages_dev)
    ranks_all = page_ranks(owners_all)
    own_owners = lax.dynamic_index_in_dim(owners_all, ctx_index, 0, keepdims=False)
    own_ranks = lax.dynamic_index_in_dim(ranks_all, ctx_index, 0, keepdims=False)
    owner_hit = jnp.arange(ctx_count)[:, None, None] == own_owners[None, None, :]
    rank_hit = jnp.arange(cap_pages)[None, :, None] == own_ranks[None, None, :]
    send_mask = jnp.logical_and(owner_hit, rank_hit).astype(jnp.bfloat16)
    send_pages = jnp.einsum(
        "oci,iskt->ocskt", send_mask, quantized, preferred_element_type=jnp.float32
    ).astype(jnp.bfloat16)
    send_scales = jnp.einsum(
        "oci,isg->ocsg", send_mask, scale_part, preferred_element_type=jnp.float32
    ).astype(jnp.bfloat16)
    got_pages, got_scales = (
        lax.all_to_all(send_pages, "ctx", split_axis=0, concat_axis=0, tiled=True),
        lax.all_to_all(send_scales, "ctx", split_axis=0, concat_axis=0, tiled=True),
    )
    to_owner = (owners_all == ctx_index)[None, :, None, :]
    rank_match = (ranks_all[:, None, :] == jnp.arange(cap_pages)[None, :, None])[None]
    slot_match = slots_all[None, :, None, :] == jnp.arange(slot_count)[:, None, None, None]
    placement = jnp.sum(
        jnp.logical_and(jnp.logical_and(to_owner, rank_match), slot_match).astype(jnp.float32),
        axis=3,
    ).astype(jnp.bfloat16)
    kv_cache = jnp.einsum(
        "lsc,scakt->lakt", placement, got_pages, preferred_element_type=jnp.float32
    ).astype(jnp.bfloat16)
    kv_scale = jnp.einsum(
        "lsc,scag->lag", placement, got_scales, preferred_element_type=jnp.float32
    ).astype(jnp.bfloat16)
    return (mixer_out, kv_cache, kv_scale)


def solution(mesh):
    in_specs = (
        P("ctx", "head"),
        P("head", None),
        P("head", None),
        P("ctx", "head"),
        P("ctx", "head"),
        P("ctx", None),
        P("ctx", None),
        P("head", "ctx"),
        P("head"),
        P("head"),
        P(),
    )
    out_specs = (P("ctx", "head"), P("ctx", None, "head", None), P("ctx", None, "head"))
    return jax.shard_map(body, mesh=mesh, in_specs=in_specs, out_specs=out_specs, check_vma=False)
```

```python
import functools
import jax
import jax.numpy as jnp
from jax import lax
from jax.sharding import PartitionSpec as P
from jax.experimental import pallas as pl
from jax.experimental.pallas import tpu as pltpu

NH = 128
P_SIZE = 64
SPAN = 256
HD = 128
PAGE = 256
GROUP = 64


LOG2E = 1.4426950408889634
F32 = jnp.float32


def lanes_of_pair(columns, p, lane_low):
    rows = columns.shape[0]
    first = jnp.broadcast_to(columns[:, 2 * p : 2 * p + 1], (rows, 2 * P_SIZE))
    second = jnp.broadcast_to(columns[:, 2 * p + 1 : 2 * p + 2], (rows, 2 * P_SIZE))
    return jnp.where(lane_low, first, second)


MESH = pl.DeviceIdType.MESH


def block_kernel(
    nw, hc, nctx, attn_h, *refs
):
    w_hs = refs[:nw]
    (x_h, g_h, b_ref, c_ref, col_ref, row_ref, decay_ref, total_ref, skip_ref, gain_ref,
     out_h, kv_ref,
     attn, w_vs, x_v, xs, xr, lr, cs, gated, run, st_own, st, dec, sq,
     load_sem, xs_sem, xr_sem, ls_sem, lr_sem, st_sem, st_rsem, de_sem, de_rsem, sq_sem, sq_rsem,
     out_sem) = refs[nw:]
    q = lax.axis_index("ctx")
    me = lax.axis_index("head")
    zc = hc // 2
    z, core = me // 2, me % 2
    rows, width = x_v.shape
    spans = rows // SPAN
    heads = col_ref.shape[1]

    loads = [pltpu.make_async_copy(attn_h, attn, load_sem.at[0])]
    loads += [pltpu.make_async_copy(w_hs[i], w_vs.at[i], load_sem.at[1 + i]) for i in range(nw)]
    load_x = pltpu.make_async_copy(x_h, x_v, load_sem.at[4])
    load_g = pltpu.make_async_copy(g_h, attn, load_sem.at[5])
    for one in loads:
        one.start()
    load_x.start()

    barrier = pltpu.get_barrier_semaphore()
    for i in range(1, hc):
        pl.semaphore_signal(barrier, inc=1, device_id=(q, lax.rem(me + i, hc)), device_id_type=MESH)
    for i in range(1, nctx):
        pl.semaphore_signal(barrier, inc=1, device_id=(lax.rem(q + i, nctx), me), device_id_type=MESH)
    pl.semaphore_wait(barrier, hc + nctx - 2)
    for one in loads:
        one.wait()

    def tile(k):
        return pl.ds(pl.multiple_of(k * SPAN, SPAN), SPAN)

    def product(dest, dst, kind):
        at = pl.ds(pl.multiple_of(dest * 128, 128), 128)
        w = jnp.concatenate([w_vs[i, :, at] for i in range(nw)], axis=1)

        def step(k, _):
            dst[tile(k), :] = jnp.dot(attn[tile(k), :], w, preferred_element_type=F32).astype(kind)
            return 0

        lax.fori_loop(0, spans, step, 0)

    def pair_copy(t):
        return pltpu.make_async_remote_copy(
            src_ref=xs.at[t], dst_ref=xr.at[t], send_sem=xs_sem.at[t], recv_sem=xr_sem.at[t],
            device_id=(q, 2 * z + 1 - core), device_id_type=MESH)

    def line_copy(t, slot, near):
        return pltpu.make_async_remote_copy(
            src_ref=xs.at[t], dst_ref=lr.at[slot], send_sem=ls_sem.at[t], recv_sem=lr_sem.at[slot],
            device_id=(q, 2 * near + core), device_id_type=MESH)

    def send_up(t):
        line_copy(t, t, z + 1).start()

    def send_down(t):
        line_copy(t, jnp.where(t == z - 1, zc, t), z - 1).start()

    for n in range(zc):
        t = jnp.where(z < zc // 2, zc - 1 - n, n)
        product(2 * t + 1 - core, xs.at[t], jnp.bfloat16)
        pair_copy(t).start()
        product(2 * t + core, cs.at[t], F32)
        pair_copy(t).wait()

        def add(k, _):
            total = cs[t, tile(k), :] + xr[t, tile(k), :].astype(F32)
            cs[t, tile(k), :] = total
            xs[t, tile(k), :] = total.astype(jnp.bfloat16)
            return 0

        lax.fori_loop(0, spans, add, 0)

        @pl.when((z == 0) & (t != z))
        def _():
            send_up(t)

        @pl.when((z == zc - 1) & (t != z))
        def _():
            send_down(t)

    load_g.start()
    load_x.wait()

    def forward(e):
        def pass_on(t):
            line_copy(t, t, z).wait_recv()

            def add(k, _):
                xs[t, tile(k), :] = (cs[t, tile(k), :] + lr[t, tile(k), :].astype(F32)).astype(jnp.bfloat16)
                return 0

            lax.fori_loop(0, spans, add, 0)

        @pl.when((z >= 1) & (z <= e))
        def _():
            t = zc - 1 - e + z
            pass_on(t)
            send_up(t)

        zm = zc - 1 - z

        @pl.when((zm >= 1) & (zm <= e))
        def _():
            t = e - zm
            pass_on(t)
            send_down(t)

    lane_low = lax.broadcasted_iota(jnp.int32, (SPAN, 2 * P_SIZE), 1) < P_SIZE

    def advance(k, p, at, x, weights, b_t):
        decayed = (x * lanes_of_pair(weights, p, lane_low)).astype(jnp.bfloat16)
        part = jnp.dot(b_t, decayed, preferred_element_type=F32)
        run[:, at] = run[:, at] * decay_ref[k, :, at] + part

    run[...] = jnp.zeros_like(run)

    def state_span(k, _):
        cum = col_ref[tile(k), :]
        weights = jnp.exp2(cum[SPAN - 1 :, :] - cum)
        b_t = b_ref[tile(k), :].T
        for p in range(heads // 2):
            at = slice(p * 2 * P_SIZE, (p + 1) * 2 * P_SIZE)
            advance(k, p, at, x_v[tile(k), at].astype(F32), weights, b_t)
        return 0

    lax.fori_loop(0, spans, state_span, 0)
    st_own[...] = run[...].astype(jnp.bfloat16)
    dec[0] = total_ref[...]

    def state_copies(i):
        to = (lax.rem(q + i, nctx), me)
        return (
            pltpu.make_async_remote_copy(
                src_ref=st_own, dst_ref=st.at[i - 1], send_sem=st_sem.at[i - 1],
                recv_sem=st_rsem.at[i - 1], device_id=to, device_id_type=MESH),
            pltpu.make_async_remote_copy(
                src_ref=dec.at[0], dst_ref=dec.at[i], send_sem=de_sem.at[i - 1],
                recv_sem=de_rsem.at[i - 1], device_id=to, device_id_type=MESH),
        )

    for i in range(1, nctx):
        @pl.when(q + i < nctx)
        def _():
            for one in state_copies(i):
                one.start()

    u_at = lax.broadcasted_iota(jnp.int32, (SPAN, SPAN), 1)
    t_at = lax.broadcasted_iota(jnp.int32, (SPAN, SPAN), 0)

    def diag_span(k, _):
        cross = lax.dot_general(
            c_ref[tile(k), :], b_ref[tile(k), :], (((1,), (1,)), ((), ())), preferred_element_type=F32)
        cross = jnp.where(u_at <= t_at, cross, 0.0)
        cum = col_ref[tile(k), :]
        for p in range(heads // 2):
            at = slice(p * 2 * P_SIZE, (p + 1) * 2 * P_SIZE)
            x = x_v[tile(k), at].astype(F32)
            out = skip_ref[:, at] * x
            for i in range(2):
                h = 2 * p + i
                spread = jnp.minimum(cum[:, h : h + 1] - row_ref[h : h + 1, tile(k)], 0.0)
                mixing = (cross * jnp.exp2(spread)).astype(jnp.bfloat16)
                mine = jnp.where(lane_low == (i == 0), x, 0.0).astype(jnp.bfloat16)
                out += jnp.dot(mixing, mine, preferred_element_type=F32)
            gated[tile(k), at] = out
        return 0

    cut = (spans * 3) // 4
    lax.fori_loop(0, cut, diag_span, 0)
    for e in range(1, zc // 2):
        forward(e)
    lax.fori_loop(cut, spans, diag_span, 0)

    run[...] = jnp.zeros_like(run)
    for i in range(nctx - 1, 0, -1):
        @pl.when(q - i >= 0)
        def _():
            for one in state_copies(i):
                one.wait_recv()
            run[...] = run[...] * dec[i, 0:1, :] + st[i - 1].astype(F32)

    load_g.wait()

    def carry_span(k, _):
        cum = col_ref[tile(k), :]
        weights = jnp.exp2(cum[SPAN - 1 :, :] - cum)
        leaving = jnp.exp2(cum)
        b_t = b_ref[tile(k), :].T
        c = c_ref[tile(k), :]
        squares = jnp.zeros((SPAN, 2 * P_SIZE), F32)
        for p in range(heads // 2):
            at = slice(p * 2 * P_SIZE, (p + 1) * 2 * P_SIZE)
            entering = run[:, at].astype(jnp.bfloat16)
            out = gated[tile(k), at] + lanes_of_pair(leaving, p, lane_low) * jnp.dot(
                c, entering, preferred_element_type=F32)
            gate = attn[tile(k), at].astype(F32)
            out = out * (gate / (1.0 + jnp.exp2(gate * -LOG2E)))
            gated[tile(k), at] = out
            squares += out * out
            advance(k, p, at, x_v[tile(k), at].astype(F32), weights, b_t)
        sq[0, :, tile(k)] = jnp.broadcast_to(jnp.sum(squares.T, axis=0, keepdims=True), (8, SPAN))
        return 0

    lax.fori_loop(0, spans, carry_span, 0)

    def square_copy(i):
        return pltpu.make_async_remote_copy(
            src_ref=sq.at[0], dst_ref=sq.at[i], send_sem=sq_sem.at[i - 1], recv_sem=sq_rsem.at[i - 1],
            device_id=(q, lax.rem(me + i, hc)), device_id_type=MESH)

    for i in range(1, hc):
        square_copy(i).start()
    for e in range(zc // 2, zc - 1):
        forward(e)
    for i in range(1, hc):
        square_copy(i).wait_recv()

    def norm_span(k, _):
        total = sq[0, 0:1, tile(k)]
        for i in range(1, hc):
            total += sq[i, 0:1, tile(k)]
        scale = lax.rsqrt(total / (NH * P_SIZE) + 1e-05)
        scale = jnp.broadcast_to(scale, (128, SPAN)).T
        for p in range(width // 128):
            at = slice(p * 128, (p + 1) * 128)
            x_v[tile(k), at] = (gated[tile(k), at] * scale * gain_ref[:, at]).astype(jnp.bfloat16)
        return 0

    lax.fori_loop(0, spans, norm_span, 0)
    store = pltpu.make_async_copy(x_v, out_h, out_sem)
    store.start()

    @pl.when(z > 0)
    def _():
        line_copy(z, z, z).wait_recv()

    @pl.when(z < zc - 1)
    def _():
        line_copy(z, zc, z).wait_recv()

    def last(k, extra):
        total = cs[z, tile(k), :]
        for slot in extra:
            total = total + lr[slot, tile(k), :].astype(F32)
        kv_ref[:, tile(k)] = total.T

    for cond, extra in ((z == 0, (zc,)), (z == zc - 1, (z,)), ((z > 0) & (z < zc - 1), (z, zc))):
        @pl.when(cond)
        def _():
            def step(k, _):
                last(k, extra)
                return 0

            lax.fori_loop(0, spans, step, 0)

    for t in range(zc):
        @pl.when(t != z)
        def _():
            line_copy(t, t, z).wait_send()
    for i in range(1, hc):
        square_copy(i).wait_send()
    for i in range(1, nctx):
        @pl.when(q + i < nctx)
        def _():
            for one in state_copies(i):
                one.wait_send()
    store.wait()


def page_ranks(owner_rows):
    count = owner_rows.shape[-1]
    same = owner_rows[..., :, None] == owner_rows[..., None, :]
    earlier = jnp.arange(count)[None, :] < jnp.arange(count)[:, None]
    return jnp.sum(jnp.logical_and(same, earlier).astype(jnp.int32), axis=-1)


def body(attn_in, w_key, w_value, ssm_in, gate, in_b, in_c, rate, skip, gain, page_table):
    tok_rows, width = ssm_in.shape
    heads_local = rate.shape[0]
    state_dim = in_b.shape[1]
    head_count = lax.axis_size("head")
    ctx_count = lax.axis_size("ctx")
    spans = tok_rows // SPAN
    kv_width = w_key.shape[1] // head_count
    feature_rows = w_key.shape[0]
    if kv_width % 128 == 0:
        weights = (w_key, w_value)
    else:
        shape = (feature_rows, head_count, kv_width)
        weights = (
            jnp.stack((w_key.reshape(shape), w_value.reshape(shape)), axis=2).reshape(
                feature_rows, head_count * 2 * kv_width
            ),
        )
    nw = len(weights)
    chunk = 2 * kv_width
    zc = head_count // 2

    upto = (jnp.arange(SPAN)[:, None] <= jnp.arange(SPAN)[None, :]).astype(F32)
    cum = jnp.einsum(
        "hcu,ut->hct", rate.reshape(heads_local, spans, SPAN) * -LOG2E, upto,
        precision=lax.Precision.HIGHEST,
    )
    span_total = cum[:, :, -1]
    cum_row = cum.reshape(heads_local, tok_rows)
    cum_col = cum_row.T
    decay = jnp.repeat(jnp.exp2(span_total), P_SIZE, axis=0).T.reshape(spans, 1, width)
    total = jnp.repeat(jnp.exp2(jnp.sum(span_total, axis=1)), P_SIZE)
    total = jnp.broadcast_to(total[None, :], (8, width))
    hbm = pl.BlockSpec(memory_space=pl.ANY)
    vmem = pl.BlockSpec(memory_space=pltpu.VMEM)
    bf16 = jnp.bfloat16
    dma = pltpu.SemaphoreType.DMA
    mixer_out, kv_rows = pl.pallas_call(
        functools.partial(block_kernel, nw, head_count, ctx_count),
        in_specs=[hbm] * (nw + 3) + [vmem] * 8,
        out_specs=[hbm, vmem],
        out_shape=[
            jax.ShapeDtypeStruct((tok_rows, width), bf16),
            jax.ShapeDtypeStruct((chunk, tok_rows), F32),
        ],
        scratch_shapes=[
            pltpu.VMEM((tok_rows, width), bf16),
            pltpu.VMEM((nw,) + weights[0].shape, bf16),
            pltpu.VMEM((tok_rows, width), bf16),
            pltpu.VMEM((zc, tok_rows, chunk), bf16),
            pltpu.VMEM((zc, tok_rows, chunk), bf16),
            pltpu.VMEM((zc + 1, tok_rows, chunk), bf16),
            pltpu.VMEM((zc, tok_rows, chunk), F32),
            pltpu.VMEM((tok_rows, width), F32),
            pltpu.VMEM((state_dim, width), F32),
            pltpu.VMEM((state_dim, width), bf16),
            pltpu.VMEM((ctx_count - 1, state_dim, width), bf16),
            pltpu.VMEM((ctx_count, 8, width), F32),
            pltpu.VMEM((head_count, 8, tok_rows), F32),
            dma((6,)),
            dma((zc,)), dma((zc,)), dma((zc,)), dma((zc + 1,)),
            dma((ctx_count - 1,)), dma((ctx_count - 1,)), dma((ctx_count - 1,)), dma((ctx_count - 1,)),
            dma((head_count - 1,)), dma((head_count - 1,)),
            dma,
        ],
        compiler_params=pltpu.CompilerParams(
            vmem_limit_bytes=60 * 1024 * 1024, collective_id=0, has_side_effects=True
        ),
        cost_estimate=pl.CostEstimate(flops=5 * 10**10, bytes_accessed=40 * 2**20, transcendentals=10**7),
    )(attn_in, *weights, ssm_in, gate, in_b, in_c, cum_col, cum_row, decay, total,
      jnp.repeat(skip, P_SIZE).reshape(1, width), gain.reshape(1, width))
    pages_dev = tok_rows // PAGE
    groups = kv_width // GROUP
    by_page = kv_rows.reshape(2, kv_width, pages_dev, PAGE).transpose(2, 0, 1, 3)
    grouped = by_page.reshape(pages_dev, 2, groups, GROUP, PAGE)
    page_max = jnp.max(jnp.abs(grouped), axis=(3, 4))
    quantized = (grouped / (page_max[..., None, None] + 1e-06)).astype(jnp.bfloat16)
    quantized = quantized.reshape(pages_dev, 2, kv_width, PAGE)
    scale_part = page_max.astype(jnp.bfloat16)
    cap_pages = (pages_dev + ctx_count - 1) // ctx_count
    slot_count = min(ctx_count * cap_pages, 2 * pages_dev)
    ctx_index = lax.axis_index("ctx")
    kv_head = lax.axis_index("head") * kv_width // HD
    head_table = lax.dynamic_index_in_dim(page_table, kv_head, 1, keepdims=False)
    owners_all = head_table[:, 0].reshape(ctx_count, pages_dev)
    slots_all = head_table[:, 1].reshape(ctx_count, pages_dev)
    ranks_all = page_ranks(owners_all)
    own_owners = lax.dynamic_index_in_dim(owners_all, ctx_index, 0, keepdims=False)
    own_ranks = lax.dynamic_index_in_dim(ranks_all, ctx_index, 0, keepdims=False)
    owner_hit = jnp.arange(ctx_count)[:, None, None] == own_owners[None, None, :]
    rank_hit = jnp.arange(cap_pages)[None, :, None] == own_ranks[None, None, :]
    send_mask = jnp.logical_and(owner_hit, rank_hit).astype(jnp.bfloat16)
    send_pages = jnp.einsum(
        "oci,iskt->ocskt", send_mask, quantized, preferred_element_type=jnp.float32
    ).astype(jnp.bfloat16)
    send_scales = jnp.einsum(
        "oci,isg->ocsg", send_mask, scale_part, preferred_element_type=jnp.float32
    ).astype(jnp.bfloat16)
    got_pages, got_scales = (
        lax.all_to_all(send_pages, "ctx", split_axis=0, concat_axis=0, tiled=True),
        lax.all_to_all(send_scales, "ctx", split_axis=0, concat_axis=0, tiled=True),
    )
    to_owner = (owners_all == ctx_index)[None, :, None, :]
    rank_match = (ranks_all[:, None, :] == jnp.arange(cap_pages)[None, :, None])[None]
    slot_match = slots_all[None, :, None, :] == jnp.arange(slot_count)[:, None, None, None]
    placement = jnp.sum(
        jnp.logical_and(jnp.logical_and(to_owner, rank_match), slot_match).astype(jnp.float32),
        axis=3,
    ).astype(jnp.bfloat16)
    kv_cache = jnp.einsum(
        "lsc,scakt->lakt", placement, got_pages, preferred_element_type=jnp.float32
    ).astype(jnp.bfloat16)
    kv_scale = jnp.einsum(
        "lsc,scag->lag", placement, got_scales, preferred_element_type=jnp.float32
    ).astype(jnp.bfloat16)
    return (mixer_out, kv_cache, kv_scale)


def solution(mesh):
    in_specs = (
        P("ctx", "head"),
        P("head", None),
        P("head", None),
        P("ctx", "head"),
        P("ctx", "head"),
        P("ctx", None),
        P("ctx", None),
        P("head", "ctx"),
        P("head"),
        P("head"),
        P(),
    )
    out_specs = (P("ctx", "head"), P("ctx", None, "head", None), P("ctx", None, "head"))
    return jax.shard_map(body, mesh=mesh, in_specs=in_specs, out_specs=out_specs, check_vma=False)
```

```python
import functools
import jax
import jax.numpy as jnp
from jax import lax
from jax.sharding import PartitionSpec as P
from jax.experimental import pallas as pl
from jax.experimental.pallas import tpu as pltpu

NH = 128
P_SIZE = 64
SPAN = 256
HD = 128
PAGE = 256
GROUP = 64


LOG2E = 1.4426950408889634
F32 = jnp.float32


def lanes_of_pair(columns, p, lane_low):
    rows = columns.shape[0]
    first = jnp.broadcast_to(columns[:, 2 * p : 2 * p + 1], (rows, 2 * P_SIZE))
    second = jnp.broadcast_to(columns[:, 2 * p + 1 : 2 * p + 2], (rows, 2 * P_SIZE))
    return jnp.where(lane_low, first, second)


MESH = pl.DeviceIdType.MESH


def block_kernel(
    nw, hc, nctx, attn_h, *refs
):
    w_hs = refs[:nw]
    (x_h, g_h, b_ref, c_ref, col_ref, row_ref, decay_ref, total_ref, skip_ref, gain_ref, idx_ref, sel_ref, pick_ref, valid_ref,
     out_h, cache_ref, scale_ref,
     attn, w_vs, x_v, xs, xr, lr, cs, gated, run, st_own, st, dec, sq, pages, going, came, scales,
     load_sem, xs_sem, xr_sem, ls_sem, lr_sem, st_sem, st_rsem, de_sem, de_rsem, sq_sem, sq_rsem,
     pg_sem, pg_rsem, sc_sem, sc_rsem, out_sem) = refs[nw:]
    q = lax.axis_index("ctx")
    me = lax.axis_index("head")
    zc = hc // 2
    z, core = me // 2, me % 2
    rows, width = x_v.shape
    spans = rows // SPAN
    heads = col_ref.shape[1]

    loads = [pltpu.make_async_copy(attn_h, attn, load_sem.at[0])]
    loads += [pltpu.make_async_copy(w_hs[i], w_vs.at[i], load_sem.at[1 + i]) for i in range(nw)]
    load_x = pltpu.make_async_copy(x_h, x_v, load_sem.at[4])
    load_g = pltpu.make_async_copy(g_h, attn, load_sem.at[5])
    for one in loads:
        one.start()
    load_x.start()

    barrier = pltpu.get_barrier_semaphore()
    for i in range(1, hc):
        pl.semaphore_signal(barrier, inc=1, device_id=(q, lax.rem(me + i, hc)), device_id_type=MESH)
    for i in range(1, nctx):
        pl.semaphore_signal(barrier, inc=1, device_id=(lax.rem(q + i, nctx), me), device_id_type=MESH)
    pl.semaphore_wait(barrier, hc + nctx - 2)
    for one in loads:
        one.wait()

    def tile(k):
        return pl.ds(pl.multiple_of(k * SPAN, SPAN), SPAN)

    def product(dest, dst, kind):
        at = pl.ds(pl.multiple_of(dest * 128, 128), 128)
        w = jnp.concatenate([w_vs[i, :, at] for i in range(nw)], axis=1)

        def step(k, _):
            dst[tile(k), :] = jnp.dot(attn[tile(k), :], w, preferred_element_type=F32).astype(kind)
            return 0

        lax.fori_loop(0, spans, step, 0)

    def pair_copy(t):
        return pltpu.make_async_remote_copy(
            src_ref=xs.at[t], dst_ref=xr.at[t], send_sem=xs_sem.at[t], recv_sem=xr_sem.at[t],
            device_id=(q, 2 * z + 1 - core), device_id_type=MESH)

    def line_copy(t, slot, near):
        return pltpu.make_async_remote_copy(
            src_ref=xs.at[t], dst_ref=lr.at[slot], send_sem=ls_sem.at[t], recv_sem=lr_sem.at[slot],
            device_id=(q, 2 * near + core), device_id_type=MESH)

    def send_up(t):
        line_copy(t, t, z + 1).start()

    def send_down(t):
        line_copy(t, jnp.where(t == z - 1, zc, t), z - 1).start()

    for n in range(zc):
        t = jnp.where(z < zc // 2, zc - 1 - n, n)
        product(2 * t + 1 - core, xs.at[t], jnp.bfloat16)
        pair_copy(t).start()
        product(2 * t + core, cs.at[t], F32)
        pair_copy(t).wait()

        def add(k, _):
            total = cs[t, tile(k), :] + xr[t, tile(k), :].astype(F32)
            cs[t, tile(k), :] = total
            xs[t, tile(k), :] = total.astype(jnp.bfloat16)
            return 0

        lax.fori_loop(0, spans, add, 0)

        @pl.when((z == 0) & (t != z))
        def _():
            send_up(t)

        @pl.when((z == zc - 1) & (t != z))
        def _():
            send_down(t)

    load_g.start()
    load_x.wait()

    def forward(e):
        def pass_on(t):
            line_copy(t, t, z).wait_recv()

            def add(k, _):
                xs[t, tile(k), :] = (cs[t, tile(k), :] + lr[t, tile(k), :].astype(F32)).astype(jnp.bfloat16)
                return 0

            lax.fori_loop(0, spans, add, 0)

        @pl.when((z >= 1) & (z <= e))
        def _():
            t = zc - 1 - e + z
            pass_on(t)
            send_up(t)

        zm = zc - 1 - z

        @pl.when((zm >= 1) & (zm <= e))
        def _():
            t = e - zm
            pass_on(t)
            send_down(t)

    lane_low = lax.broadcasted_iota(jnp.int32, (SPAN, 2 * P_SIZE), 1) < P_SIZE

    def advance(k, p, at, x, weights, b_t):
        decayed = (x * lanes_of_pair(weights, p, lane_low)).astype(jnp.bfloat16)
        part = jnp.dot(b_t, decayed, preferred_element_type=F32)
        run[:, at] = run[:, at] * decay_ref[k, :, at] + part

    run[...] = jnp.zeros_like(run)

    def state_span(k, _):
        cum = col_ref[tile(k), :]
        weights = jnp.exp2(cum[SPAN - 1 :, :] - cum)
        b_t = b_ref[tile(k), :].T
        for p in range(heads // 2):
            at = slice(p * 2 * P_SIZE, (p + 1) * 2 * P_SIZE)
            advance(k, p, at, x_v[tile(k), at].astype(F32), weights, b_t)
        return 0

    lax.fori_loop(0, spans, state_span, 0)
    st_own[...] = run[...].astype(jnp.bfloat16)
    dec[0] = total_ref[...]

    def state_copies(i):
        to = (lax.rem(q + i, nctx), me)
        return (
            pltpu.make_async_remote_copy(
                src_ref=st_own, dst_ref=st.at[i - 1], send_sem=st_sem.at[i - 1],
                recv_sem=st_rsem.at[i - 1], device_id=to, device_id_type=MESH),
            pltpu.make_async_remote_copy(
                src_ref=dec.at[0], dst_ref=dec.at[i], send_sem=de_sem.at[i - 1],
                recv_sem=de_rsem.at[i - 1], device_id=to, device_id_type=MESH),
        )

    for i in range(1, nctx):
        @pl.when(q + i < nctx)
        def _():
            for one in state_copies(i):
                one.start()

    u_at = lax.broadcasted_iota(jnp.int32, (SPAN, SPAN), 1)
    t_at = lax.broadcasted_iota(jnp.int32, (SPAN, SPAN), 0)

    def diag_span(k, _):
        cross = lax.dot_general(
            c_ref[tile(k), :], b_ref[tile(k), :], (((1,), (1,)), ((), ())), preferred_element_type=F32)
        cross = jnp.where(u_at <= t_at, cross, 0.0)
        cum = col_ref[tile(k), :]
        for p in range(heads // 2):
            at = slice(p * 2 * P_SIZE, (p + 1) * 2 * P_SIZE)
            x = x_v[tile(k), at].astype(F32)
            out = skip_ref[:, at] * x
            for i in range(2):
                h = 2 * p + i
                spread = jnp.minimum(cum[:, h : h + 1] - row_ref[h : h + 1, tile(k)], 0.0)
                mixing = (cross * jnp.exp2(spread)).astype(jnp.bfloat16)
                mine = jnp.where(lane_low == (i == 0), x, 0.0).astype(jnp.bfloat16)
                out += jnp.dot(mixing, mine, preferred_element_type=F32)
            gated[tile(k), at] = out
        return 0

    cut = (spans * 3) // 4
    lax.fori_loop(0, cut, diag_span, 0)
    for e in range(1, zc // 2):
        forward(e)
    lax.fori_loop(cut, spans, diag_span, 0)

    run[...] = jnp.zeros_like(run)
    for i in range(nctx - 1, 0, -1):
        @pl.when(q - i >= 0)
        def _():
            for one in state_copies(i):
                one.wait_recv()
            run[...] = run[...] * dec[i, 0:1, :] + st[i - 1].astype(F32)

    load_g.wait()

    def carry_span(k, _):
        cum = col_ref[tile(k), :]
        weights = jnp.exp2(cum[SPAN - 1 :, :] - cum)
        leaving = jnp.exp2(cum)
        b_t = b_ref[tile(k), :].T
        c = c_ref[tile(k), :]
        squares = jnp.zeros((SPAN, 2 * P_SIZE), F32)
        for p in range(heads // 2):
            at = slice(p * 2 * P_SIZE, (p + 1) * 2 * P_SIZE)
            entering = run[:, at].astype(jnp.bfloat16)
            out = gated[tile(k), at] + lanes_of_pair(leaving, p, lane_low) * jnp.dot(
                c, entering, preferred_element_type=F32)
            gate = attn[tile(k), at].astype(F32)
            out = out * (gate / (1.0 + jnp.exp2(gate * -LOG2E)))
            gated[tile(k), at] = out
            squares += out * out
            advance(k, p, at, x_v[tile(k), at].astype(F32), weights, b_t)
        sq[0, :, tile(k)] = jnp.broadcast_to(jnp.sum(squares.T, axis=0, keepdims=True), (8, SPAN))
        return 0

    lax.fori_loop(0, spans, carry_span, 0)

    def square_copy(i):
        return pltpu.make_async_remote_copy(
            src_ref=sq.at[0], dst_ref=sq.at[i], send_sem=sq_sem.at[i - 1], recv_sem=sq_rsem.at[i - 1],
            device_id=(q, lax.rem(me + i, hc)), device_id_type=MESH)

    for i in range(1, hc):
        square_copy(i).start()
    for e in range(zc // 2, zc - 1):
        forward(e)
    for i in range(1, hc):
        square_copy(i).wait_recv()

    def norm_span(k, _):
        total = sq[0, 0:1, tile(k)]
        for i in range(1, hc):
            total += sq[i, 0:1, tile(k)]
        scale = lax.rsqrt(total / (NH * P_SIZE) + 1e-05)
        scale = jnp.broadcast_to(scale, (128, SPAN)).T
        for p in range(width // 128):
            at = slice(p * 128, (p + 1) * 128)
            x_v[tile(k), at] = (gated[tile(k), at] * scale * gain_ref[:, at]).astype(jnp.bfloat16)
        return 0

    lax.fori_loop(0, spans, norm_span, 0)
    store = pltpu.make_async_copy(x_v, out_h, out_sem)
    store.start()

    @pl.when(z > 0)
    def _():
        line_copy(z, z, z).wait_recv()

    @pl.when(z < zc - 1)
    def _():
        line_copy(z, zc, z).wait_recv()

    def last(k, extra):
        total = cs[z, tile(k), :]
        for slot in extra:
            total = total + lr[slot, tile(k), :].astype(F32)
        by_column = total.T
        scales[nctx - 1, k] = jnp.zeros((8, 128), F32)
        for g in range(by_column.shape[0] // GROUP):
            at = slice(g * GROUP, (g + 1) * GROUP)
            part = by_column[at, :]
            most = jnp.max(jnp.max(jnp.abs(part), axis=0, keepdims=True), axis=1, keepdims=True)
            pages[k, at, :] = (part / (most + 1e-06)).astype(jnp.bfloat16)
            scales[nctx - 1, k, g : g + 1, :] = jnp.broadcast_to(most, (1, 128))

    for cond, extra in ((z == 0, (zc,)), (z == zc - 1, (z,)), ((z > 0) & (z < zc - 1), (z, zc))):
        @pl.when(cond)
        def _():
            def step(k, _):
                last(k, extra)
                return 0

            lax.fori_loop(0, spans, step, 0)

    cap = idx_ref.shape[1]

    def page_copies(i):
        to = (lax.rem(q + i, nctx), me)
        return (
            pltpu.make_async_remote_copy(
                src_ref=going.at[i - 1], dst_ref=came.at[i - 1], send_sem=pg_sem.at[i - 1],
                recv_sem=pg_rsem.at[i - 1], device_id=to, device_id_type=MESH),
            pltpu.make_async_remote_copy(
                src_ref=scales.at[nctx - 1], dst_ref=scales.at[i - 1], send_sem=sc_sem.at[i - 1],
                recv_sem=sc_rsem.at[i - 1], device_id=to, device_id_type=MESH),
        )

    for i in range(1, nctx):
        for n in range(cap):
            going[i - 1, n] = pages[idx_ref[lax.rem(q + i, nctx), n]]
        for one in page_copies(i):
            one.start()
    for n in range(cap):
        came[nctx - 1, n] = pages[idx_ref[q, n]]
    for t in range(zc):
        @pl.when(t != z)
        def _():
            line_copy(t, t, z).wait_send()
    for i in range(1, hc):
        square_copy(i).wait_send()
    for i in range(1, nctx):
        @pl.when(q + i < nctx)
        def _():
            for one in state_copies(i):
                one.wait_send()
    for i in range(1, nctx):
        for one in page_copies(i):
            one.wait()
    for n in range(cache_ref.shape[0]):
        keep = valid_ref[n]
        page = came[sel_ref[n, 0], sel_ref[n, 1]].astype(F32) * keep
        cache_ref[n] = page.astype(jnp.bfloat16)
        scale_ref[n] = scales[pick_ref[n, 0], pick_ref[n, 1]] * keep
    store.wait()


def page_ranks(owner_rows):
    count = owner_rows.shape[-1]
    same = owner_rows[..., :, None] == owner_rows[..., None, :]
    earlier = jnp.arange(count)[None, :] < jnp.arange(count)[:, None]
    return jnp.sum(jnp.logical_and(same, earlier).astype(jnp.int32), axis=-1)


def body(attn_in, w_key, w_value, ssm_in, gate, in_b, in_c, rate, skip, gain, page_table):
    tok_rows, width = ssm_in.shape
    heads_local = rate.shape[0]
    state_dim = in_b.shape[1]
    head_count = lax.axis_size("head")
    ctx_count = lax.axis_size("ctx")
    spans = tok_rows // SPAN
    kv_width = w_key.shape[1] // head_count
    feature_rows = w_key.shape[0]
    if kv_width % 128 == 0:
        weights = (w_key, w_value)
    else:
        shape = (feature_rows, head_count, kv_width)
        weights = (
            jnp.stack((w_key.reshape(shape), w_value.reshape(shape)), axis=2).reshape(
                feature_rows, head_count * 2 * kv_width
            ),
        )
    nw = len(weights)
    chunk = 2 * kv_width
    zc = head_count // 2

    upto = (jnp.arange(SPAN)[:, None] <= jnp.arange(SPAN)[None, :]).astype(F32)
    cum = jnp.einsum(
        "hcu,ut->hct", rate.reshape(heads_local, spans, SPAN) * -LOG2E, upto,
        precision=lax.Precision.HIGHEST,
    )
    span_total = cum[:, :, -1]
    cum_row = cum.reshape(heads_local, tok_rows)
    cum_col = cum_row.T
    decay = jnp.repeat(jnp.exp2(span_total), P_SIZE, axis=0).T.reshape(spans, 1, width)
    total = jnp.repeat(jnp.exp2(jnp.sum(span_total, axis=1)), P_SIZE)
    total = jnp.broadcast_to(total[None, :], (8, width))
    hbm = pl.BlockSpec(memory_space=pl.ANY)
    vmem = pl.BlockSpec(memory_space=pltpu.VMEM)
    bf16 = jnp.bfloat16
    dma = pltpu.SemaphoreType.DMA
    pages_dev = tok_rows // PAGE
    groups = kv_width // GROUP
    cap_pages = (pages_dev + ctx_count - 1) // ctx_count
    slot_count = min(ctx_count * cap_pages, 2 * pages_dev)
    ctx_index = lax.axis_index("ctx")
    kv_head = lax.axis_index("head") * kv_width // HD
    head_table = lax.dynamic_index_in_dim(page_table, kv_head, 1, keepdims=False)
    owners_all = head_table[:, 0].reshape(ctx_count, pages_dev)
    slots_all = head_table[:, 1].reshape(ctx_count, pages_dev)
    ranks_all = page_ranks(owners_all)
    own_owners = lax.dynamic_index_in_dim(owners_all, ctx_index, 0, keepdims=False)
    own_ranks = lax.dynamic_index_in_dim(ranks_all, ctx_index, 0, keepdims=False)
    owner_hit = jnp.arange(ctx_count)[:, None, None] == own_owners[None, None, :]
    rank_hit = jnp.arange(cap_pages)[None, :, None] == own_ranks[None, None, :]
    page_at = jnp.arange(pages_dev, dtype=jnp.int32)
    leaving = jnp.sum(jnp.where(owner_hit & rank_hit, page_at[None, None, :], 0), axis=2)
    apart = (ctx_index - jnp.arange(ctx_count, dtype=jnp.int32)) % ctx_count
    place = jnp.where(apart == 0, ctx_count - 1, apart - 1)
    here = (owners_all == ctx_index)[None] & (
        slots_all[None] == jnp.arange(slot_count)[:, None, None]
    )

    def chosen(values):
        values = jnp.broadcast_to(values, owners_all.shape)[None]
        return jnp.sum(jnp.where(here, values, 0), axis=(1, 2)).astype(jnp.int32)

    select = jnp.stack([chosen(place[:, None]), chosen(ranks_all)], axis=1)
    pick = jnp.stack([chosen(place[:, None]), chosen(page_at[None, :])], axis=1)
    filled = jnp.sum(here.astype(F32), axis=(1, 2))
    smem = pl.BlockSpec(memory_space=pltpu.SMEM)
    mixer_out, kv_cache, scales = pl.pallas_call(
        functools.partial(block_kernel, nw, head_count, ctx_count),
        in_specs=[hbm] * (nw + 3) + [vmem] * 8 + [smem] * 4,
        out_specs=[hbm, vmem, vmem],
        out_shape=[
            jax.ShapeDtypeStruct((tok_rows, width), bf16),
            jax.ShapeDtypeStruct((slot_count, chunk, PAGE), bf16),
            jax.ShapeDtypeStruct((slot_count, 8, 128), F32),
        ],
        scratch_shapes=[
            pltpu.VMEM((tok_rows, width), bf16),
            pltpu.VMEM((nw,) + weights[0].shape, bf16),
            pltpu.VMEM((tok_rows, width), bf16),
            pltpu.VMEM((zc, tok_rows, chunk), bf16),
            pltpu.VMEM((zc, tok_rows, chunk), bf16),
            pltpu.VMEM((zc + 1, tok_rows, chunk), bf16),
            pltpu.VMEM((zc, tok_rows, chunk), F32),
            pltpu.VMEM((tok_rows, width), F32),
            pltpu.VMEM((state_dim, width), F32),
            pltpu.VMEM((state_dim, width), bf16),
            pltpu.VMEM((ctx_count - 1, state_dim, width), bf16),
            pltpu.VMEM((ctx_count, 8, width), F32),
            pltpu.VMEM((head_count, 8, tok_rows), F32),
            pltpu.VMEM((pages_dev, chunk, PAGE), bf16),
            pltpu.VMEM((ctx_count - 1, cap_pages, chunk, PAGE), bf16),
            pltpu.VMEM((ctx_count, cap_pages, chunk, PAGE), bf16),
            pltpu.VMEM((ctx_count, pages_dev, 8, 128), F32),
            dma((6,)),
            dma((zc,)), dma((zc,)), dma((zc,)), dma((zc + 1,)),
            dma((ctx_count - 1,)), dma((ctx_count - 1,)), dma((ctx_count - 1,)), dma((ctx_count - 1,)),
            dma((head_count - 1,)), dma((head_count - 1,)),
            dma((ctx_count - 1,)), dma((ctx_count - 1,)), dma((ctx_count - 1,)), dma((ctx_count - 1,)),
            dma,
        ],
        compiler_params=pltpu.CompilerParams(
            vmem_limit_bytes=60 * 1024 * 1024, collective_id=0, has_side_effects=True
        ),
        cost_estimate=pl.CostEstimate(flops=5 * 10**10, bytes_accessed=40 * 2**20, transcendentals=10**7),
    )(attn_in, *weights, ssm_in, gate, in_b, in_c, cum_col, cum_row, decay, total,
      jnp.repeat(skip, P_SIZE).reshape(1, width), gain.reshape(1, width),
      leaving.astype(jnp.int32), select, pick, filled)
    kv_cache = kv_cache.reshape(slot_count, 2, kv_width, PAGE)
    kv_scale = scales[:, : 2 * groups, 0].astype(bf16).reshape(slot_count, 2, groups)
    return (mixer_out, kv_cache, kv_scale)


def solution(mesh):
    in_specs = (
        P("ctx", "head"),
        P("head", None),
        P("head", None),
        P("ctx", "head"),
        P("ctx", "head"),
        P("ctx", None),
        P("ctx", None),
        P("head", "ctx"),
        P("head"),
        P("head"),
        P(),
    )
    out_specs = (P("ctx", "head"), P("ctx", None, "head", None), P("ctx", None, "head"))
    return jax.shard_map(body, mesh=mesh, in_specs=in_specs, out_specs=out_specs, check_vma=False)
```

```python
import functools
import jax
import jax.numpy as jnp
from jax import lax
from jax.sharding import PartitionSpec as P
from jax.experimental import pallas as pl
from jax.experimental.pallas import tpu as pltpu

NH = 128
P_SIZE = 64
SPAN = 256
HD = 128
PAGE = 256
GROUP = 64


LOG2E = 1.4426950408889634
F32 = jnp.float32


def lanes_of_pair(columns, p, lane_low):
    rows = columns.shape[0]
    first = jnp.broadcast_to(columns[:, 2 * p : 2 * p + 1], (rows, 2 * P_SIZE))
    second = jnp.broadcast_to(columns[:, 2 * p + 1 : 2 * p + 2], (rows, 2 * P_SIZE))
    return jnp.where(lane_low, first, second)


MESH = pl.DeviceIdType.MESH


def block_kernel(
    nw, hc, nctx, attn_h, *refs
):
    w_hs = refs[:nw]
    (x_h, g_h, b_ref, c_ref, col_ref, row_ref, decay_ref, total_ref, skip_ref, gain_ref, idx_ref, sel_ref, pick_ref, valid_ref,
     out_h, cache_ref, scale_ref,
     attn, w_vs, x_v, xs, xr, lr, cs, gated, run, st_own, st, dec, sq, pages, going, came, scales,
     load_sem, xs_sem, xr_sem, ls_sem, lr_sem, st_sem, st_rsem, de_sem, de_rsem, sq_sem, sq_rsem,
     pg_sem, pg_rsem, sc_sem, sc_rsem, out_sem) = refs[nw:]
    q = lax.axis_index("ctx")
    me = lax.axis_index("head")
    zc = hc // 2
    z, core = me // 2, me % 2
    rows, width = x_v.shape
    spans = rows // SPAN
    heads = col_ref.shape[1]

    loads = [pltpu.make_async_copy(attn_h, attn, load_sem.at[0])]
    loads += [pltpu.make_async_copy(w_hs[i], w_vs.at[i], load_sem.at[1 + i]) for i in range(nw)]
    load_x = pltpu.make_async_copy(x_h, x_v, load_sem.at[4])
    load_g = pltpu.make_async_copy(g_h, attn, load_sem.at[5])
    for one in loads:
        one.start()
    load_x.start()

    barrier = pltpu.get_barrier_semaphore()
    for i in range(1, hc):
        pl.semaphore_signal(barrier, inc=1, device_id=(q, lax.rem(me + i, hc)), device_id_type=MESH)
    for i in range(1, nctx):
        pl.semaphore_signal(barrier, inc=1, device_id=(lax.rem(q + i, nctx), me), device_id_type=MESH)
    pl.semaphore_wait(barrier, hc + nctx - 2)
    for one in loads:
        one.wait()

    def tile(k):
        return pl.ds(pl.multiple_of(k * SPAN, SPAN), SPAN)

    def product(dest, dst, kind):
        at = pl.ds(pl.multiple_of(dest * 128, 128), 128)
        w = jnp.concatenate([w_vs[i, :, at] for i in range(nw)], axis=1)

        def step(k, _):
            dst[tile(k), :] = jnp.dot(attn[tile(k), :], w, preferred_element_type=F32).astype(kind)
            return 0

        lax.fori_loop(0, spans, step, 0)

    def pair_copy(t):
        return pltpu.make_async_remote_copy(
            src_ref=xs.at[t], dst_ref=xr.at[t], send_sem=xs_sem.at[t], recv_sem=xr_sem.at[t],
            device_id=(q, 2 * z + 1 - core), device_id_type=MESH)

    def line_copy(t, slot, near):
        return pltpu.make_async_remote_copy(
            src_ref=xs.at[t], dst_ref=lr.at[slot], send_sem=ls_sem.at[t], recv_sem=lr_sem.at[slot],
            device_id=(q, 2 * near + core), device_id_type=MESH)

    def send_up(t):
        line_copy(t, t, z + 1).start()

    def send_down(t):
        line_copy(t, jnp.where(t == z - 1, zc, t), z - 1).start()

    for n in range(zc):
        t = jnp.where(z < zc // 2, zc - 1 - n, n)
        product(2 * t + 1 - core, xs.at[t], jnp.bfloat16)
        pair_copy(t).start()
        product(2 * t + core, cs.at[t], F32)
        pair_copy(t).wait()

        def add(k, _):
            total = cs[t, tile(k), :] + xr[t, tile(k), :].astype(F32)
            cs[t, tile(k), :] = total
            xs[t, tile(k), :] = total.astype(jnp.bfloat16)
            return 0

        lax.fori_loop(0, spans, add, 0)

        @pl.when((z == 0) & (t != z))
        def _():
            send_up(t)

        @pl.when((z == zc - 1) & (t != z))
        def _():
            send_down(t)

    load_g.start()
    load_x.wait()

    def forward(e):
        def pass_on(t):
            line_copy(t, t, z).wait_recv()

            def add(k, _):
                xs[t, tile(k), :] = (cs[t, tile(k), :] + lr[t, tile(k), :].astype(F32)).astype(jnp.bfloat16)
                return 0

            lax.fori_loop(0, spans, add, 0)

        @pl.when((z >= 1) & (z <= e))
        def _():
            t = zc - 1 - e + z
            pass_on(t)
            send_up(t)

        zm = zc - 1 - z

        @pl.when((zm >= 1) & (zm <= e))
        def _():
            t = e - zm
            pass_on(t)
            send_down(t)

    lane_low = lax.broadcasted_iota(jnp.int32, (SPAN, 2 * P_SIZE), 1) < P_SIZE

    def advance(k, p, at, x, weights, b_t):
        decayed = (x * lanes_of_pair(weights, p, lane_low)).astype(jnp.bfloat16)
        part = jnp.dot(b_t, decayed, preferred_element_type=F32)
        run[:, at] = run[:, at] * decay_ref[k, :, at] + part

    run[...] = jnp.zeros_like(run)

    def state_span(k, _):
        cum = col_ref[tile(k), :]
        weights = jnp.exp2(cum[SPAN - 1 :, :] - cum)
        b_t = b_ref[tile(k), :].T
        for p in range(heads // 2):
            at = slice(p * 2 * P_SIZE, (p + 1) * 2 * P_SIZE)
            advance(k, p, at, x_v[tile(k), at].astype(F32), weights, b_t)
        return 0

    lax.fori_loop(0, spans, state_span, 0)
    st_own[...] = run[...].astype(jnp.bfloat16)
    dec[0] = total_ref[...]

    def state_copies(i):
        to = (lax.rem(q + i, nctx), me)
        return (
            pltpu.make_async_remote_copy(
                src_ref=st_own, dst_ref=st.at[i - 1], send_sem=st_sem.at[i - 1],
                recv_sem=st_rsem.at[i - 1], device_id=to, device_id_type=MESH),
            pltpu.make_async_remote_copy(
                src_ref=dec.at[0], dst_ref=dec.at[i], send_sem=de_sem.at[i - 1],
                recv_sem=de_rsem.at[i - 1], device_id=to, device_id_type=MESH),
        )

    for i in range(1, nctx):
        @pl.when(q + i < nctx)
        def _():
            for one in state_copies(i):
                one.start()

    u_at = lax.broadcasted_iota(jnp.int32, (SPAN, SPAN), 1)
    t_at = lax.broadcasted_iota(jnp.int32, (SPAN, SPAN), 0)

    def diag_span(k, _):
        cross = lax.dot_general(
            c_ref[tile(k), :], b_ref[tile(k), :], (((1,), (1,)), ((), ())), preferred_element_type=F32)
        cross = jnp.where(u_at <= t_at, cross, 0.0)
        cum = col_ref[tile(k), :]
        for p in range(heads // 2):
            at = slice(p * 2 * P_SIZE, (p + 1) * 2 * P_SIZE)
            x = x_v[tile(k), at].astype(F32)
            out = skip_ref[:, at] * x
            for i in range(2):
                h = 2 * p + i
                spread = jnp.minimum(cum[:, h : h + 1] - row_ref[h : h + 1, tile(k)], 0.0)
                mixing = (cross * jnp.exp2(spread)).astype(jnp.bfloat16)
                mine = jnp.where(lane_low == (i == 0), x, 0.0).astype(jnp.bfloat16)
                out += jnp.dot(mixing, mine, preferred_element_type=F32)
            gated[tile(k), at] = out
        return 0

    cut = spans // 8
    lax.fori_loop(0, cut, diag_span, 0)
    for e in range(1, zc // 2):
        forward(e)
    lax.fori_loop(cut, spans, diag_span, 0)

    run[...] = jnp.zeros_like(run)
    for i in range(nctx - 1, 0, -1):
        @pl.when(q - i >= 0)
        def _():
            for one in state_copies(i):
                one.wait_recv()
            run[...] = run[...] * dec[i, 0:1, :] + st[i - 1].astype(F32)

    load_g.wait()

    def carry_span(k, _):
        cum = col_ref[tile(k), :]
        weights = jnp.exp2(cum[SPAN - 1 :, :] - cum)
        leaving = jnp.exp2(cum)
        b_t = b_ref[tile(k), :].T
        c = c_ref[tile(k), :]
        squares = jnp.zeros((SPAN, 2 * P_SIZE), F32)
        for p in range(heads // 2):
            at = slice(p * 2 * P_SIZE, (p + 1) * 2 * P_SIZE)
            entering = run[:, at].astype(jnp.bfloat16)
            out = gated[tile(k), at] + lanes_of_pair(leaving, p, lane_low) * jnp.dot(
                c, entering, preferred_element_type=F32)
            gate = attn[tile(k), at].astype(F32)
            out = out * (gate / (1.0 + jnp.exp2(gate * -LOG2E)))
            gated[tile(k), at] = out
            squares += out * out
            advance(k, p, at, x_v[tile(k), at].astype(F32), weights, b_t)
        sq[0, :, tile(k)] = jnp.broadcast_to(jnp.sum(squares.T, axis=0, keepdims=True), (8, SPAN))
        return 0

    lax.fori_loop(0, spans, carry_span, 0)

    def square_copy(i):
        return pltpu.make_async_remote_copy(
            src_ref=sq.at[0], dst_ref=sq.at[i], send_sem=sq_sem.at[i - 1], recv_sem=sq_rsem.at[i - 1],
            device_id=(q, lax.rem(me + i, hc)), device_id_type=MESH)

    for i in range(1, hc):
        square_copy(i).start()
    for e in range(zc // 2, zc - 1):
        forward(e)
    for i in range(1, hc):
        square_copy(i).wait_recv()

    def norm_span(k, _):
        total = sq[0, 0:1, tile(k)]
        for i in range(1, hc):
            total += sq[i, 0:1, tile(k)]
        scale = lax.rsqrt(total / (NH * P_SIZE) + 1e-05)
        scale = jnp.broadcast_to(scale, (128, SPAN)).T
        for p in range(width // 128):
            at = slice(p * 128, (p + 1) * 128)
            x_v[tile(k), at] = (gated[tile(k), at] * scale * gain_ref[:, at]).astype(jnp.bfloat16)
        return 0

    lax.fori_loop(0, spans, norm_span, 0)
    store = pltpu.make_async_copy(x_v, out_h, out_sem)
    store.start()

    @pl.when(z > 0)
    def _():
        line_copy(z, z, z).wait_recv()

    @pl.when(z < zc - 1)
    def _():
        line_copy(z, zc, z).wait_recv()

    def last(k, extra):
        total = cs[z, tile(k), :]
        for slot in extra:
            total = total + lr[slot, tile(k), :].astype(F32)
        by_column = total.T
        scales[nctx - 1, k] = jnp.zeros((8, 128), F32)
        for g in range(by_column.shape[0] // GROUP):
            at = slice(g * GROUP, (g + 1) * GROUP)
            part = by_column[at, :]
            most = jnp.max(jnp.max(jnp.abs(part), axis=0, keepdims=True), axis=1, keepdims=True)
            pages[k, at, :] = (part / (most + 1e-06)).astype(jnp.bfloat16)
            scales[nctx - 1, k, g : g + 1, :] = jnp.broadcast_to(most, (1, 128))

    for cond, extra in ((z == 0, (zc,)), (z == zc - 1, (z,)), ((z > 0) & (z < zc - 1), (z, zc))):
        @pl.when(cond)
        def _():
            def step(k, _):
                last(k, extra)
                return 0

            lax.fori_loop(0, spans, step, 0)

    cap = idx_ref.shape[1]

    def page_copies(i):
        to = (lax.rem(q + i, nctx), me)
        return (
            pltpu.make_async_remote_copy(
                src_ref=going.at[i - 1], dst_ref=came.at[i - 1], send_sem=pg_sem.at[i - 1],
                recv_sem=pg_rsem.at[i - 1], device_id=to, device_id_type=MESH),
            pltpu.make_async_remote_copy(
                src_ref=scales.at[nctx - 1], dst_ref=scales.at[i - 1], send_sem=sc_sem.at[i - 1],
                recv_sem=sc_rsem.at[i - 1], device_id=to, device_id_type=MESH),
        )

    for i in range(1, nctx):
        for n in range(cap):
            going[i - 1, n] = pages[idx_ref[lax.rem(q + i, nctx), n]]
        for one in page_copies(i):
            one.start()
    for n in range(cap):
        came[nctx - 1, n] = pages[idx_ref[q, n]]
    for t in range(zc):
        @pl.when(t != z)
        def _():
            line_copy(t, t, z).wait_send()
    for i in range(1, hc):
        square_copy(i).wait_send()
    for i in range(1, nctx):
        @pl.when(q + i < nctx)
        def _():
            for one in state_copies(i):
                one.wait_send()
    for i in range(1, nctx):
        for one in page_copies(i):
            one.wait()
    for n in range(cache_ref.shape[0]):
        keep = valid_ref[n]
        page = came[sel_ref[n, 0], sel_ref[n, 1]].astype(F32) * keep
        cache_ref[n] = page.astype(jnp.bfloat16)
        scale_ref[n] = scales[pick_ref[n, 0], pick_ref[n, 1]] * keep
    store.wait()


def page_ranks(owner_rows):
    count = owner_rows.shape[-1]
    same = owner_rows[..., :, None] == owner_rows[..., None, :]
    earlier = jnp.arange(count)[None, :] < jnp.arange(count)[:, None]
    return jnp.sum(jnp.logical_and(same, earlier).astype(jnp.int32), axis=-1)


def body(attn_in, w_key, w_value, ssm_in, gate, in_b, in_c, rate, skip, gain, page_table):
    tok_rows, width = ssm_in.shape
    heads_local = rate.shape[0]
    state_dim = in_b.shape[1]
    head_count = lax.axis_size("head")
    ctx_count = lax.axis_size("ctx")
    spans = tok_rows // SPAN
    kv_width = w_key.shape[1] // head_count
    feature_rows = w_key.shape[0]
    if kv_width % 128 == 0:
        weights = (w_key, w_value)
    else:
        shape = (feature_rows, head_count, kv_width)
        weights = (
            jnp.stack((w_key.reshape(shape), w_value.reshape(shape)), axis=2).reshape(
                feature_rows, head_count * 2 * kv_width
            ),
        )
    nw = len(weights)
    chunk = 2 * kv_width
    zc = head_count // 2

    upto = (jnp.arange(SPAN)[:, None] <= jnp.arange(SPAN)[None, :]).astype(F32)
    cum = jnp.einsum(
        "hcu,ut->hct", rate.reshape(heads_local, spans, SPAN) * -LOG2E, upto,
        precision=lax.Precision.HIGHEST,
    )
    span_total = cum[:, :, -1]
    cum_row = cum.reshape(heads_local, tok_rows)
    cum_col = cum_row.T
    decay = jnp.repeat(jnp.exp2(span_total), P_SIZE, axis=0).T.reshape(spans, 1, width)
    total = jnp.repeat(jnp.exp2(jnp.sum(span_total, axis=1)), P_SIZE)
    total = jnp.broadcast_to(total[None, :], (8, width))
    hbm = pl.BlockSpec(memory_space=pl.ANY)
    vmem = pl.BlockSpec(memory_space=pltpu.VMEM)
    bf16 = jnp.bfloat16
    dma = pltpu.SemaphoreType.DMA
    pages_dev = tok_rows // PAGE
    groups = kv_width // GROUP
    cap_pages = (pages_dev + ctx_count - 1) // ctx_count
    slot_count = min(ctx_count * cap_pages, 2 * pages_dev)
    ctx_index = lax.axis_index("ctx")
    kv_head = lax.axis_index("head") * kv_width // HD
    head_table = lax.dynamic_index_in_dim(page_table, kv_head, 1, keepdims=False)
    owners_all = head_table[:, 0].reshape(ctx_count, pages_dev)
    slots_all = head_table[:, 1].reshape(ctx_count, pages_dev)
    ranks_all = page_ranks(owners_all)
    own_owners = lax.dynamic_index_in_dim(owners_all, ctx_index, 0, keepdims=False)
    own_ranks = lax.dynamic_index_in_dim(ranks_all, ctx_index, 0, keepdims=False)
    owner_hit = jnp.arange(ctx_count)[:, None, None] == own_owners[None, None, :]
    rank_hit = jnp.arange(cap_pages)[None, :, None] == own_ranks[None, None, :]
    page_at = jnp.arange(pages_dev, dtype=jnp.int32)
    leaving = jnp.sum(jnp.where(owner_hit & rank_hit, page_at[None, None, :], 0), axis=2)
    apart = (ctx_index - jnp.arange(ctx_count, dtype=jnp.int32)) % ctx_count
    place = jnp.where(apart == 0, ctx_count - 1, apart - 1)
    here = (owners_all == ctx_index)[None] & (
        slots_all[None] == jnp.arange(slot_count)[:, None, None]
    )

    def chosen(values):
        values = jnp.broadcast_to(values, owners_all.shape)[None]
        return jnp.sum(jnp.where(here, values, 0), axis=(1, 2)).astype(jnp.int32)

    select = jnp.stack([chosen(place[:, None]), chosen(ranks_all)], axis=1)
    pick = jnp.stack([chosen(place[:, None]), chosen(page_at[None, :])], axis=1)
    filled = jnp.sum(here.astype(F32), axis=(1, 2))
    smem = pl.BlockSpec(memory_space=pltpu.SMEM)
    mixer_out, kv_cache, scales = pl.pallas_call(
        functools.partial(block_kernel, nw, head_count, ctx_count),
        in_specs=[hbm] * (nw + 3) + [vmem] * 8 + [smem] * 4,
        out_specs=[hbm, vmem, vmem],
        out_shape=[
            jax.ShapeDtypeStruct((tok_rows, width), bf16),
            jax.ShapeDtypeStruct((slot_count, chunk, PAGE), bf16),
            jax.ShapeDtypeStruct((slot_count, 8, 128), F32),
        ],
        scratch_shapes=[
            pltpu.VMEM((tok_rows, width), bf16),
            pltpu.VMEM((nw,) + weights[0].shape, bf16),
            pltpu.VMEM((tok_rows, width), bf16),
            pltpu.VMEM((zc, tok_rows, chunk), bf16),
            pltpu.VMEM((zc, tok_rows, chunk), bf16),
            pltpu.VMEM((zc + 1, tok_rows, chunk), bf16),
            pltpu.VMEM((zc, tok_rows, chunk), F32),
            pltpu.VMEM((tok_rows, width), F32),
            pltpu.VMEM((state_dim, width), F32),
            pltpu.VMEM((state_dim, width), bf16),
            pltpu.VMEM((ctx_count - 1, state_dim, width), bf16),
            pltpu.VMEM((ctx_count, 8, width), F32),
            pltpu.VMEM((head_count, 8, tok_rows), F32),
            pltpu.VMEM((pages_dev, chunk, PAGE), bf16),
            pltpu.VMEM((ctx_count - 1, cap_pages, chunk, PAGE), bf16),
            pltpu.VMEM((ctx_count, cap_pages, chunk, PAGE), bf16),
            pltpu.VMEM((ctx_count, pages_dev, 8, 128), F32),
            dma((6,)),
            dma((zc,)), dma((zc,)), dma((zc,)), dma((zc + 1,)),
            dma((ctx_count - 1,)), dma((ctx_count - 1,)), dma((ctx_count - 1,)), dma((ctx_count - 1,)),
            dma((head_count - 1,)), dma((head_count - 1,)),
            dma((ctx_count - 1,)), dma((ctx_count - 1,)), dma((ctx_count - 1,)), dma((ctx_count - 1,)),
            dma,
        ],
        compiler_params=pltpu.CompilerParams(
            vmem_limit_bytes=60 * 1024 * 1024, collective_id=0, has_side_effects=True
        ),
        cost_estimate=pl.CostEstimate(flops=5 * 10**10, bytes_accessed=40 * 2**20, transcendentals=10**7),
    )(attn_in, *weights, ssm_in, gate, in_b, in_c, cum_col, cum_row, decay, total,
      jnp.repeat(skip, P_SIZE).reshape(1, width), gain.reshape(1, width),
      leaving.astype(jnp.int32), select, pick, filled)
    kv_cache = kv_cache.reshape(slot_count, 2, kv_width, PAGE)
    kv_scale = scales[:, : 2 * groups, 0].astype(bf16).reshape(slot_count, 2, groups)
    return (mixer_out, kv_cache, kv_scale)


def solution(mesh):
    in_specs = (
        P("ctx", "head"),
        P("head", None),
        P("head", None),
        P("ctx", "head"),
        P("ctx", "head"),
        P("ctx", None),
        P("ctx", None),
        P("head", "ctx"),
        P("head"),
        P("head"),
        P(),
    )
    out_specs = (P("ctx", "head"), P("ctx", None, "head", None), P("ctx", None, "head"))
    return jax.shard_map(body, mesh=mesh, in_specs=in_specs, out_specs=out_specs, check_vma=False)
```
